32 devices in a mesh: dp: 16 (over z, y, core), seq: 2 (over x).
Axes of the slice: x: 2, y: 2, z: 4, core: 2. Of those that a mesh axis runs over, the one named last changes fastest.
Arguments:
- tile_feats: bfloat16 [8192, 2048], P('dp'), may hold values from -6 to 6
- tile_pos: int32 [16, 512], P('dp'), may hold values from -1 to 511, as said below
- slide_count: int32 [16], P('dp'), may hold values from 128 to 512, as said below
- w_proj: bfloat16 [2048, 768], P(None, 'seq'), may hold values from -0.125 to 0.125
- emb_grad: bfloat16 [16, 512, 768], P('dp', 'seq'), may hold values from -6 to 6
- ln_gain: float32 [768], replicated, may hold values from 0.25 to 1.75
- w_qkv: bfloat16 [768, 2304], P('dp'), may hold values from -1.5 to 1.5
- w_out: bfloat16 [768, 768], P('dp'), may hold values from -0.21875 to 0.21875
Outputs:
- slide_emb: bfloat16 [16, 512, 768], P('dp', 'seq')
- attn_branch: bfloat16 [16, 512, 768], P('dp', 'seq')
- proj_grad: float32 [2048, 768], P(None, 'seq')
The draws below stay inside these ranges and needn't reach their ends.
Inputs may be any that keep to these rules, and one draw needn't show every extreme that they name: `tile_pos`: slot j of a row belongs to slide j // 32. Each position below a slide's slide_count is held by exactly one slot of that slide over all rows; all other slots hold -1. `slide_count`: some slide is full.
All inputs are finite; a program needn't handle non-finite values.
Results may differ from the reference program's by a relative error of at most 0.017.
The reference program's roundings to bfloat16 on the way (of `emb_tiles`, `normed`, `projected`, `context` and `slot_grad`) count: a program that leaves them out, or rounds other values in their place, can miss the bound.
Values may be sent and summed in bfloat16 or wider, within the bound.
A program may use at most 128 MiB of HBM per device.

```python
import jax
import jax.numpy as jnp
from jax import lax

FEAT = 2048
D = 768
HEAD_COUNT = 12
HEAD_WIDTH = 64
DILATION_STEP = 4
SEQ_DEV = 256
SLIDES = 16
SLIDE_LENGTH = 512
MOST = 32
SLOTS = 512
N_SEQ = 2


def slide_layout(key):
    base = jax.random.fold_in(key, 11)
    count_key, pick_key, order_key = jax.random.split(base, 3)
    counts = jax.random.randint(count_key, (SLIDES,), SLIDE_LENGTH // 4, SLIDE_LENGTH + 1)
    chosen = jax.random.randint(pick_key, (), 0, SLIDES)
    counts = jnp.where(jnp.arange(SLIDES) == chosen, SLIDE_LENGTH, counts).astype(jnp.int32)
    order_keys = jax.random.split(order_key, SLIDES)

    def one_order(single_key):
        return jax.random.permutation(single_key, SLIDE_LENGTH)
    orders = jax.vmap(one_order)(order_keys).astype(jnp.int32)
    return (counts, orders)


def draw_slide_count(key, part):
    return slide_layout(key)[0]


def draw_tile_pos(key, part):
    counts, orders = slide_layout(key)
    placed = jnp.where(orders < counts[:, None], orders, -1)
    grouped = placed.reshape(SLIDES, SLIDES, MOST).transpose(1, 0, 2)
    return grouped.reshape(SLIDES, SLOTS).astype(jnp.int32)


def draw_w_qkv(key, part):
    bound_value = (3.0 / D) ** 0.5
    values = jax.random.uniform(jax.random.fold_in(key, 5), (D, 3 * HEAD_COUNT * HEAD_WIDTH), jnp.float32, -bound_value, bound_value)
    return values.astype(jnp.bfloat16)


def level_of(rng, dims, cuts, smallest, high):
    def one(dim, blocks):
        draws = jax.random.uniform(jax.random.fold_in(jax.random.fold_in(rng, 6), dim), (blocks,), jnp.float32, smallest / len(cuts), high / len(cuts))
        return jnp.repeat(jnp.exp(draws), dims[dim] // blocks).reshape((-1,) + (1,) * (len(dims) - dim - 1))

    factor_of = one(*cuts[0])
    for cut in cuts[1:]:
        factor_of = factor_of * one(*cut)
    return factor_of


def normal_values(key, extent, deviation, limit, pieces=(), held_as=jnp.bfloat16):
    level = level_of(key, extent, pieces, -0.22, 0.18) if pieces else 1.0
    result = jax.random.normal(key, extent, jnp.float32) * deviation * level
    return jnp.minimum(jnp.maximum(result, -limit), limit).astype(held_as)


def setup_inputs(seed: int = 0) -> dict:
    streams_of = jax.random.split(jax.random.key(seed), 9)
    return {
        "tile_feats": normal_values(streams_of[0], (SLIDES * SLOTS, FEAT), 1.0, 6.0, ((0, 16),)),
        "tile_pos": draw_tile_pos(jax.random.fold_in(streams_of[8], 71), 0),
        "slide_count": draw_slide_count(jax.random.fold_in(streams_of[8], 71), 0),
        "w_proj": normal_values(streams_of[3], (FEAT, D), FEAT ** -0.5, 0.125, ((1, 2),)),
        "emb_grad": normal_values(streams_of[4], (SLIDES, SLIDE_LENGTH, D), 1.0, 6.0, ((0, 16), (1, 2))),
        "ln_gain": jnp.clip(1.0 + 0.15 * jax.random.normal(streams_of[5], (D,), jnp.float32), 0.25, 1.75),
        "w_qkv": draw_w_qkv(jax.random.fold_in(streams_of[8], 71), 0),
        "w_out": normal_values(streams_of[7], (HEAD_COUNT * HEAD_WIDTH, D), (HEAD_COUNT * HEAD_WIDTH) ** -0.5, 0.21875, ((0, 16),)),
    }


NEGATIVE = -1e+30
EPSILON = 1e-05

def attend_slide(slide_rows, tile_count, ln_gain, w_qkv, w_out):
    inner = HEAD_COUNT * HEAD_WIDTH
    scale = HEAD_WIDTH ** (-0.5)
    widened = slide_rows.astype(jnp.float32)
    center = lax.optimization_barrier(jnp.mean(widened, axis=-1, keepdims=True))
    spread = lax.optimization_barrier(jnp.mean(jnp.square(widened - center), axis=-1, keepdims=True))
    normed = ((widened - center) * lax.rsqrt(spread + EPSILON) * ln_gain).astype(jnp.bfloat16)
    projected = jnp.dot(normed, w_qkv, preferred_element_type=jnp.float32).astype(jnp.bfloat16)
    query_rows = projected[:, :inner].reshape(SLIDE_LENGTH, HEAD_COUNT, HEAD_WIDTH).astype(jnp.float32)
    key_matrix = projected[:, inner:2 * inner].reshape(SLIDE_LENGTH, HEAD_COUNT, HEAD_WIDTH).astype(jnp.float32)
    value_matrix = projected[:, 2 * inner:].reshape(SLIDE_LENGTH, HEAD_COUNT, HEAD_WIDTH).astype(jnp.float32)
    sequence_position = jnp.arange(SLIDE_LENGTH, dtype=jnp.int32)
    occupied = sequence_position < tile_count
    shift_amounts = jnp.arange(HEAD_COUNT, dtype=jnp.int32) % DILATION_STEP
    permitted_mask = sequence_position[None, :] % DILATION_STEP == shift_amounts[:, None]
    block_q = query_rows.reshape(N_SEQ, SEQ_DEV, HEAD_COUNT, HEAD_WIDTH)
    block_k = key_matrix.reshape(N_SEQ, SEQ_DEV, HEAD_COUNT, HEAD_WIDTH)
    block_v = value_matrix.reshape(N_SEQ, SEQ_DEV, HEAD_COUNT, HEAD_WIDTH)
    local_scores = jnp.einsum('bqhd,bkhd->hbqk', block_q, block_k) * scale
    local_ok = jnp.broadcast_to(occupied.reshape(N_SEQ, SEQ_DEV)[None, :, None, :], local_scores.shape)
    local_scores = local_scores.reshape(HEAD_COUNT, SLIDE_LENGTH, SEQ_DEV)
    local_ok = local_ok.reshape(HEAD_COUNT, SLIDE_LENGTH, SEQ_DEV)
    stepped_keys = key_matrix.reshape(SLIDE_LENGTH // DILATION_STEP, DILATION_STEP, HEAD_COUNT, HEAD_WIDTH)
    stepped_values = value_matrix.reshape(SLIDE_LENGTH // DILATION_STEP, DILATION_STEP, HEAD_COUNT, HEAD_WIDTH)
    distant_keys = jnp.stack([stepped_keys[:, head_number % DILATION_STEP, head_number, :] for head_number in range(HEAD_COUNT)])
    distant_values = jnp.stack([stepped_values[:, head_number % DILATION_STEP, head_number, :] for head_number in range(HEAD_COUNT)])
    distant_position = DILATION_STEP * jnp.arange(SLIDE_LENGTH // DILATION_STEP, dtype=jnp.int32)[None, :] + shift_amounts[:, None]
    far_scores = jnp.einsum('qhd,hkd->hqk', query_rows, distant_keys) * scale
    far_ok = (distant_position < tile_count)[:, None, :] & permitted_mask[:, :, None]
    maxima = jnp.maximum(lax.optimization_barrier(jnp.max(jnp.where(local_ok, local_scores, NEGATIVE), axis=-1)), lax.optimization_barrier(jnp.max(jnp.where(far_ok, far_scores, NEGATIVE), axis=-1)))
    local_weight = jnp.where(local_ok, jnp.exp(local_scores - maxima[..., None]), 0.0)
    far_weight = jnp.where(far_ok, jnp.exp(far_scores - maxima[..., None]), 0.0)
    totals = lax.optimization_barrier(jnp.sum(local_weight, axis=-1)) + lax.optimization_barrier(jnp.sum(far_weight, axis=-1))
    nearby_accumulator = jnp.einsum('hbqk,bkhd->hbqd', local_weight.reshape(HEAD_COUNT, N_SEQ, SEQ_DEV, SEQ_DEV), block_v)
    nearby_accumulator = nearby_accumulator.reshape(HEAD_COUNT, SLIDE_LENGTH, HEAD_WIDTH)
    far_acc = jnp.einsum('hqk,hkd->hqd', far_weight, distant_values)
    safe_totals = jnp.where(occupied[None, :], totals, 1.0)
    context = jnp.where(occupied[None, :, None], (nearby_accumulator + far_acc) / safe_totals[..., None], 0.0)
    context = context.transpose(1, 0, 2).reshape(SLIDE_LENGTH, inner).astype(jnp.bfloat16)
    return jnp.dot(context, w_out, preferred_element_type=jnp.float32).astype(jnp.bfloat16)

def reference(tile_feats, tile_pos, slide_count, w_proj, emb_grad, ln_gain, w_qkv, w_out):
    emb_tiles = jnp.dot(tile_feats, w_proj, preferred_element_type=jnp.float32).astype(jnp.bfloat16)
    slot_index = jnp.arange(SLIDES * SLOTS, dtype=jnp.int32)
    slot_slide = slot_index % SLOTS // MOST
    flat_position = tile_pos.reshape(SLIDES * SLOTS).astype(jnp.int32)
    target = jnp.where(flat_position >= 0, slot_slide * SLIDE_LENGTH + flat_position, SLIDES * SLIDE_LENGTH).astype(jnp.int32)
    placed = jnp.zeros((SLIDES * SLIDE_LENGTH + 1, D), jnp.bfloat16).at[target].set(emb_tiles)
    slide_emb = placed[:SLIDES * SLIDE_LENGTH].reshape(SLIDES, SLIDE_LENGTH, D)

    def one_slide(bundle):
        return attend_slide(bundle[0], bundle[1], ln_gain, w_qkv, w_out)
    attn_branch = lax.map(one_slide, (slide_emb, slide_count))
    grad_rows = jnp.concatenate([emb_grad.reshape(SLIDES * SLIDE_LENGTH, D), jnp.zeros((1, D), jnp.bfloat16)], axis=0)
    slot_grad = grad_rows[target]
    proj_grad = lax.dot_general(tile_feats, slot_grad, (((0,), (0,)), ((), ())), preferred_element_type=jnp.float32)
    return (slide_emb, attn_branch, proj_grad)
```

```python
import functools

import jax
import jax.numpy as jnp
from jax import lax
from jax.experimental import pallas as pl
from jax.experimental.pallas import tpu as pltpu
from jax.sharding import PartitionSpec as P

D = 768
HEAD_COUNT = 12
HEAD_WIDTH = 64
DILATION_STEP = 4
NEGATIVE = -1e30
EPSILON = 1e-05
STEP_HEADS = 4

F32 = jnp.float32
BF16 = jnp.bfloat16


def put_rows(whole, rows, low, high):
    pieces = [whole[:low]] if low else []
    pieces.append(rows)
    if high < whole.shape[0]:
        pieces.append(whole[high:])
    return jnp.concatenate(pieces, axis=0)


def attention_kernel(
    seq_count,
    nearby,
    meta_ref,
    rows_ref,
    gain_ref,
    wq_ref,
    wk_ref,
    wv_ref,
    wo_ref,
    emb_ref,
    branch_ref,
    normed,
    context,
):
    step = pl.program_id(0)
    me = meta_ref[0]
    count = meta_ref[1]
    part = nearby // DILATION_STEP
    own = pl.multiple_of(me * nearby, nearby)

    @pl.when(step == 0)
    def _():
        for block in range(seq_count):
            at = slice(block * nearby, (block + 1) * nearby)
            wide = jnp.concatenate(
                [rows_ref[c, at, :] for c in range(seq_count)], axis=-1
            ).astype(F32)
            center = jnp.mean(wide, axis=-1, keepdims=True)
            spread = jnp.mean(jnp.square(wide - center), axis=-1, keepdims=True)
            normed[at, :] = (
                (wide - center) * lax.rsqrt(spread + EPSILON) * gain_ref[...]
            ).astype(BF16)

    mine = normed[pl.ds(own, nearby), :]
    query = jnp.dot(mine, wq_ref[...], preferred_element_type=F32).astype(BF16)
    query = query * BF16(HEAD_WIDTH**-0.5)
    key = jnp.dot(mine, wk_ref[...], preferred_element_type=F32).astype(BF16)
    value = jnp.dot(mine, wv_ref[...], preferred_element_type=F32).astype(BF16)
    far_keys, far_values = [], []
    for other in range(1, seq_count):
        block = lax.rem(me + other, seq_count)
        start = pl.multiple_of(block * nearby, nearby)
        theirs = normed[pl.ds(start, nearby), :]
        far_keys.append(jnp.dot(theirs, wk_ref[...], preferred_element_type=F32).astype(BF16))
        far_values.append(jnp.dot(theirs, wv_ref[...], preferred_element_type=F32).astype(BF16))

    lane = lax.broadcasted_iota(jnp.int32, (1, nearby), 1)
    key_ok = own + (lane % part) * DILATION_STEP + lane // part < count
    row = lax.broadcasted_iota(jnp.int32, (nearby, 1), 0)
    query_ok = own + (row % part) * DILATION_STEP + row // part < count
    far_lane = lax.broadcasted_iota(jnp.int32, (1, part * (seq_count - 1)), 1)
    far_block = lax.rem(me + 1 + far_lane // part, seq_count)
    far_spot = far_block * nearby + far_lane % part * DILATION_STEP
    dims = (((1,), (1,)), ((), ()))
    outs = []
    for head in range(STEP_HEADS):
        shift = head % DILATION_STEP
        cols = slice(head * HEAD_WIDTH, (head + 1) * HEAD_WIDTH)
        low, high = shift * part, (shift + 1) * part
        q, k, v = query[:, cols], key[:, cols], value[:, cols]
        scores = lax.dot_general(q, k, dims, preferred_element_type=F32)
        scores = jnp.where(key_ok, scores, NEGATIVE)
        maximum = jnp.max(scores, axis=-1, keepdims=True)
        far_k = jnp.concatenate([x[low:high, cols] for x in far_keys], axis=0)
        far_v = jnp.concatenate([x[low:high, cols] for x in far_values], axis=0)
        far_ok = far_spot + shift < count
        far = lax.dot_general(q[low:high], far_k, dims, preferred_element_type=F32)
        far = jnp.where(far_ok, far, NEGATIVE)
        far_max = jnp.maximum(maximum[low:high], jnp.max(far, axis=-1, keepdims=True))
        maximum = put_rows(maximum, far_max, low, high)
        weight = jnp.exp(scores - maximum)
        in_lane = (lane >= low) & (lane < high)
        twice = jnp.where(in_lane, weight[low:high] * 2.0, weight[low:high])
        weight = put_rows(weight, twice, low, high)
        far_weight = jnp.exp(far - far_max)
        total = jnp.sum(weight, axis=-1, keepdims=True)
        far_total = jnp.sum(far_weight, axis=-1, keepdims=True)
        total = put_rows(total, total[low:high] + far_total, low, high)
        gathered = jnp.dot(weight.astype(BF16), v, preferred_element_type=F32)
        far_gathered = jnp.dot(far_weight.astype(BF16), far_v, preferred_element_type=F32)
        gathered = put_rows(gathered, gathered[low:high] + far_gathered, low, high)
        outs.append(jnp.where(query_ok, gathered / total, 0.0).astype(BF16))
    context[step] = jnp.concatenate(outs, axis=-1)

    @pl.when(step == pl.num_programs(0) - 1)
    def _():
        at_row = lax.broadcasted_iota(jnp.int32, (nearby, nearby), 0)
        at_lane = lax.broadcasted_iota(jnp.int32, (nearby, nearby), 1)
        natural = (at_lane % part) * DILATION_STEP + at_lane // part
        back = jnp.where(at_row == natural, 1.0, 0.0).astype(BF16)
        ordered = jnp.concatenate(
            [rows_ref[c, pl.ds(own, nearby), :] for c in range(seq_count)], axis=-1
        )
        emb_ref[...] = jnp.dot(back, ordered, preferred_element_type=F32).astype(BF16)
        whole = jnp.concatenate(
            [context[i] for i in range(HEAD_COUNT // STEP_HEADS)], axis=-1
        )
        whole = jnp.dot(back, whole, preferred_element_type=F32).astype(BF16)
        branch_ref[...] = jnp.dot(whole, wo_ref[...], preferred_element_type=F32).astype(BF16)


def attend(meta, rows, gain, w_qkv, w_out, seq_count, nearby):
    width = STEP_HEADS * HEAD_WIDTH
    steps = HEAD_COUNT // STEP_HEADS
    slide_len = rows.shape[1]
    full = lambda *shape: pl.BlockSpec(shape, lambda i: (0,) * len(shape))
    out = jax.ShapeDtypeStruct((nearby, D), BF16)
    return pl.pallas_call(
        functools.partial(attention_kernel, seq_count, nearby),
        out_shape=(out, out),
        grid=(steps,),
        in_specs=[
            pl.BlockSpec(memory_space=pltpu.SMEM),
            full(*rows.shape),
            full(1, D),
            pl.BlockSpec((D, width), lambda i: (0, i)),
            pl.BlockSpec((D, width), lambda i: (0, steps + i)),
            pl.BlockSpec((D, width), lambda i: (0, 2 * steps + i)),
            full(D, D),
        ],
        out_specs=(full(nearby, D), full(nearby, D)),
        scratch_shapes=[
            pltpu.VMEM((slide_len, D), BF16),
            pltpu.VMEM((steps, nearby, width), BF16),
        ],
        compiler_params=pltpu.CompilerParams(vmem_limit_bytes=48 * 1024 * 1024),
        cost_estimate=pl.CostEstimate(
            flops=20_000_000_000, bytes_accessed=20_000_000, transcendentals=1_000_000
        ),
    )(meta, rows, gain, w_qkv, w_qkv, w_qkv, w_out)


def local(tile_feats, tile_pos, slide_count, w_proj, emb_grad, ln_gain, w_qkv, w_out):
    seq_count = lax.axis_size("seq")
    seq_index = lax.axis_index("seq")
    slot_rows = tile_feats.shape[0]
    nearby = emb_grad.shape[1]
    slide_len = nearby * seq_count
    part = nearby // DILATION_STEP
    positions = lax.all_to_all(
        tile_pos.reshape(slot_rows), "dp", split_axis=0, concat_axis=0, tiled=True
    )
    returned_grad = lax.all_to_all(
        emb_grad.reshape(nearby, D), "seq", split_axis=1, concat_axis=0, tiled=True
    )
    spot = jnp.arange(slide_len, dtype=jnp.int32)
    hot = (spot[:, None] == positions[None, :]).astype(BF16)
    picked_grad = lax.dot_general(
        hot, returned_grad, (((0,), (0,)), ((), ())), preferred_element_type=F32
    ).astype(BF16)
    slot_grad = lax.all_to_all(picked_grad, "dp", split_axis=0, concat_axis=0, tiled=True)
    grad_part = lax.dot_general(
        tile_feats, slot_grad, (((0,), (0,)), ((), ())), preferred_element_type=F32
    )
    proj_grad = lax.psum(grad_part.astype(BF16), "dp").astype(F32)

    emb_part = jnp.dot(tile_feats, w_proj, preferred_element_type=F32).astype(BF16)
    arrived = lax.all_to_all(emb_part, "dp", split_axis=0, concat_axis=0, tiled=True)
    inside = spot % nearby
    at_spot = spot - inside + (inside % part) * DILATION_STEP + inside // part
    hot_perm = (at_spot[:, None] == positions[None, :]).astype(BF16)
    slide_rows = jnp.dot(hot_perm, arrived, preferred_element_type=F32).astype(BF16)
    rows = lax.all_gather(slide_rows, "seq", axis=0, tiled=False)
    meta = jnp.stack([seq_index.astype(jnp.int32), slide_count[0]])
    local_emb, attn_branch = attend(
        meta,
        rows,
        ln_gain.reshape(1, D),
        lax.all_gather(w_qkv, "dp", axis=0, tiled=True),
        lax.all_gather(w_out, "dp", axis=0, tiled=True),
        seq_count,
        nearby,
    )
    return (local_emb[None], attn_branch[None], proj_grad)


def solution(mesh):
    in_specs = (
        P("dp", None),
        P("dp", None),
        P("dp"),
        P(None, "seq"),
        P("dp", "seq", None),
        P(),
        P("dp", None),
        P("dp", None),
    )
    out_specs = (P("dp", "seq", None), P("dp", "seq", None), P(None, "seq"))
    return jax.shard_map(local, mesh=mesh, in_specs=in_specs, out_specs=out_specs, check_vma=False)
```

```python
import functools

import jax
import jax.numpy as jnp
from jax import lax
from jax.experimental import pallas as pl
from jax.experimental.pallas import tpu as pltpu
from jax.sharding import PartitionSpec as P

D = 768
HEAD_COUNT = 12
HEAD_WIDTH = 64
DILATION_STEP = 4
NEGATIVE = -1e30
EPSILON = 1e-05
STEP_HEADS = 4

F32 = jnp.float32
BF16 = jnp.bfloat16
MESH = pl.DeviceIdType.MESH


def greet(dp_peers, seq_peers):
    barrier = pltpu.get_barrier_semaphore()
    dp_count, seq_count = lax.axis_size("dp"), lax.axis_size("seq")
    dp, seq = lax.axis_index("dp"), lax.axis_index("seq")
    if dp_peers:

        @pl.loop(1, dp_count)
        def _(t):
            pl.semaphore_signal(
                barrier, device_id=(lax.rem(dp + t, dp_count), seq), device_id_type=MESH
            )

    if seq_peers:

        @pl.loop(1, seq_count)
        def _(t):
            pl.semaphore_signal(
                barrier, device_id=(dp, lax.rem(seq + t, seq_count)), device_id_type=MESH
            )

    pl.semaphore_wait(
        barrier, (dp_count - 1 if dp_peers else 0) + (seq_count - 1 if seq_peers else 0)
    )


def remote(src, dst, send, recv, device):
    return pltpu.make_async_remote_copy(
        src_ref=src,
        dst_ref=dst,
        send_sem=send,
        recv_sem=recv,
        device_id=device,
        device_id_type=MESH,
    )


def first_kernel(n, seq_count, pos, grad, pos_out, grad_out, ps, pr, gs, gr):
    dp, seq = lax.axis_index("dp"), lax.axis_index("seq")
    greet(True, True)

    def grad_copy(t):
        peer = lax.rem(seq + t, seq_count)
        return remote(grad.at[peer], grad_out.at[seq], gs.at[t], gr.at[t], (dp, peer))

    def pos_copy(t):
        peer = lax.rem(dp + t, n)
        return remote(pos.at[peer], pos_out.at[dp], ps.at[t], pr.at[t], (peer, seq))

    @pl.loop(1, n)
    def _(t):
        pos_copy(t).start()

    @pl.loop(1, seq_count)
    def _(t):
        grad_copy(t).start()

    pos_out[dp] = pos[dp]
    grad_out[seq] = grad[seq]

    @pl.loop(1, n)
    def _(t):
        pos_copy(t).wait()

    @pl.loop(1, seq_count)
    def _(t):
        grad_copy(t).wait()


def second_kernel(n, seq_count, emb, grad, emb_out, grad_out, es, er, gs, gr, fs, fr):
    dp, seq = lax.axis_index("dp"), lax.axis_index("seq")
    greet(True, True)

    def emb_copy(t):
        peer = lax.rem(dp + t, n)
        return remote(emb.at[peer], emb_out.at[seq, dp], es.at[t], er.at[t], (peer, seq))

    def grad_copy(t):
        peer = lax.rem(dp + t, n)
        return remote(grad.at[peer], grad_out.at[dp], gs.at[t], gr.at[t], (peer, seq))

    def forward(k, t):
        source = lax.rem(dp - t + n, n)
        peer = lax.rem(seq + k, seq_count)
        block = emb_out.at[seq, source]
        return remote(block, block, fs.at[k, t], fr.at[k, t], (dp, peer))

    @pl.loop(1, n)
    def _(t):
        emb_copy(t).start()

    @pl.loop(1, n)
    def _(t):
        grad_copy(t).start()

    emb_out[seq, dp] = emb[dp]
    grad_out[dp] = grad[dp]
    for k in range(1, seq_count):
        forward(k, 0).start()

    @pl.loop(1, n)
    def _(t):
        emb_copy(t).wait_recv()
        for k in range(1, seq_count):
            forward(k, t).start()

    @pl.loop(1, n)
    def _(t):
        grad_copy(t).wait()
        emb_copy(t).wait_send()

    @pl.loop(0, n)
    def _(t):
        for k in range(1, seq_count):
            forward(k, t).wait()


def reduce_kernel(
    n, src, out, pair, stage, arrive, s1, r1, s2, r2, s3, r3, s4, r4
):
    dp, seq = lax.axis_index("dp"), lax.axis_index("seq")
    half = n // 2
    side, group = lax.rem(dp, 2), dp // 2
    sibling = (group * 2 + 1 - side, seq)
    barrier = pltpu.get_barrier_semaphore()
    pl.semaphore_signal(barrier, device_id=sibling, device_id_type=MESH)

    @pl.loop(1, half)
    def _(t):
        pl.semaphore_signal(
            barrier,
            device_id=(lax.rem(group + t, half) * 2 + side, seq),
            device_id_type=MESH,
        )

    pl.semaphore_wait(barrier, half)

    def ahead(t):
        return lax.rem(group + t, half)

    def behind(t):
        return lax.rem(group - t + half, half)

    def to_sibling(t):
        return remote(src.at[1 - side, ahead(t)], pair.at[t], s1.at[t], r1.at[t], sibling)

    def to_owner(t):
        return remote(
            stage.at[t], arrive.at[t], s2.at[t], r2.at[t], (ahead(t) * 2 + side, seq)
        )

    def to_peer(t):
        block = out.at[side, group]
        return remote(block, block, s3.at[t], r3.at[t], (ahead(t) * 2 + side, seq))

    def hand_over(t):
        block = out.at[side, behind(t)]
        return remote(block, block, s4.at[t], r4.at[t], sibling)

    @pl.loop(1, half)
    def _(t):
        to_sibling(t).start()

    to_sibling(0).start()

    @pl.loop(1, half)
    def _(t):
        to_sibling(t).wait_recv()
        stage[t] = (src[side, ahead(t)].astype(F32) + pair[t].astype(F32)).astype(BF16)
        to_owner(t).start()

    to_sibling(0).wait_recv()
    stage[0] = (src[side, group].astype(F32) + pair[0].astype(F32)).astype(BF16)

    @pl.loop(1, half)
    def _(t):
        to_owner(t).wait_recv()

    total = stage[0].astype(F32)
    for t in range(1, half):
        total = total + arrive[t].astype(F32)
    out[side, group] = total.astype(BF16)

    @pl.loop(1, half)
    def _(t):
        to_peer(t).start()

    hand_over(0).start()

    @pl.loop(1, half)
    def _(t):
        to_peer(t).wait_recv()
        hand_over(t).start()

    @pl.loop(1, half)
    def _(t):
        to_owner(t).wait_send()
        to_peer(t).wait_send()

    @pl.loop(0, half)
    def _(t):
        to_sibling(t).wait_send()
        hand_over(t).wait()


VM = pl.BlockSpec(memory_space=pltpu.VMEM)
DMA = pltpu.SemaphoreType.DMA


def exchange(kernel, ident, outs, scratch, *operands):
    return pl.pallas_call(
        kernel,
        out_shape=tuple(jax.ShapeDtypeStruct(shape, kind) for shape, kind in outs),
        in_specs=[VM] * len(operands),
        out_specs=tuple([VM] * len(outs)),
        scratch_shapes=scratch,
        compiler_params=pltpu.CompilerParams(
            collective_id=ident, has_side_effects=True, vmem_limit_bytes=32 * 1024 * 1024
        ),
        cost_estimate=pl.CostEstimate(
            flops=10_000_000_000, bytes_accessed=10_000_000, transcendentals=0
        ),
    )(*operands)


def put_rows(whole, rows, low, high):
    pieces = [whole[:low]] if low else []
    pieces.append(rows)
    if high < whole.shape[0]:
        pieces.append(whole[high:])
    return jnp.concatenate(pieces, axis=0)


def attention_kernel(
    seq_count,
    nearby,
    meta_ref,
    rows_ref,
    gain_ref,
    wq_ref,
    wk_ref,
    wv_ref,
    wo_ref,
    emb_ref,
    branch_ref,
    normed,
    context,
):
    step = pl.program_id(0)
    me = meta_ref[0]
    count = meta_ref[1]
    part = nearby // DILATION_STEP
    own = pl.multiple_of(me * nearby, nearby)

    @pl.when(step == 0)
    def _():
        for block in range(seq_count):
            at = slice(block * nearby, (block + 1) * nearby)
            wide = jnp.concatenate(
                [rows_ref[c, at, :] for c in range(seq_count)], axis=-1
            ).astype(F32)
            center = jnp.mean(wide, axis=-1, keepdims=True)
            spread = jnp.mean(jnp.square(wide - center), axis=-1, keepdims=True)
            normed[at, :] = (
                (wide - center) * lax.rsqrt(spread + EPSILON) * gain_ref[...]
            ).astype(BF16)

    mine = normed[pl.ds(own, nearby), :]
    query = jnp.dot(mine, wq_ref[...], preferred_element_type=F32).astype(BF16)
    query = query * BF16(HEAD_WIDTH**-0.5)
    key = jnp.dot(mine, wk_ref[...], preferred_element_type=F32).astype(BF16)
    value = jnp.dot(mine, wv_ref[...], preferred_element_type=F32).astype(BF16)
    far_keys, far_values = [], []
    for other in range(1, seq_count):
        block = lax.rem(me + other, seq_count)
        start = pl.multiple_of(block * nearby, nearby)
        theirs = normed[pl.ds(start, nearby), :]
        far_keys.append(jnp.dot(theirs, wk_ref[...], preferred_element_type=F32).astype(BF16))
        far_values.append(jnp.dot(theirs, wv_ref[...], preferred_element_type=F32).astype(BF16))

    lane = lax.broadcasted_iota(jnp.int32, (1, nearby), 1)
    key_ok = own + (lane % part) * DILATION_STEP + lane // part < count
    row = lax.broadcasted_iota(jnp.int32, (nearby, 1), 0)
    query_ok = own + (row % part) * DILATION_STEP + row // part < count
    far_lane = lax.broadcasted_iota(jnp.int32, (1, part * (seq_count - 1)), 1)
    far_block = lax.rem(me + 1 + far_lane // part, seq_count)
    far_spot = far_block * nearby + far_lane % part * DILATION_STEP
    dims = (((1,), (1,)), ((), ()))
    outs = []
    for head in range(STEP_HEADS):
        shift = head % DILATION_STEP
        cols = slice(head * HEAD_WIDTH, (head + 1) * HEAD_WIDTH)
        low, high = shift * part, (shift + 1) * part
        q, k, v = query[:, cols], key[:, cols], value[:, cols]
        scores = lax.dot_general(q, k, dims, preferred_element_type=F32)
        scores = jnp.where(key_ok, scores, NEGATIVE)
        maximum = jnp.max(scores, axis=-1, keepdims=True)
        far_k = jnp.concatenate([x[low:high, cols] for x in far_keys], axis=0)
        far_v = jnp.concatenate([x[low:high, cols] for x in far_values], axis=0)
        far_ok = far_spot + shift < count
        far = lax.dot_general(q[low:high], far_k, dims, preferred_element_type=F32)
        far = jnp.where(far_ok, far, NEGATIVE)
        far_max = jnp.maximum(maximum[low:high], jnp.max(far, axis=-1, keepdims=True))
        maximum = put_rows(maximum, far_max, low, high)
        weight = jnp.exp(scores - maximum)
        in_lane = (lane >= low) & (lane < high)
        twice = jnp.where(in_lane, weight[low:high] * 2.0, weight[low:high])
        weight = put_rows(weight, twice, low, high)
        far_weight = jnp.exp(far - far_max)
        total = jnp.sum(weight, axis=-1, keepdims=True)
        far_total = jnp.sum(far_weight, axis=-1, keepdims=True)
        total = put_rows(total, total[low:high] + far_total, low, high)
        gathered = jnp.dot(weight.astype(BF16), v, preferred_element_type=F32)
        far_gathered = jnp.dot(far_weight.astype(BF16), far_v, preferred_element_type=F32)
        gathered = put_rows(gathered, gathered[low:high] + far_gathered, low, high)
        outs.append(jnp.where(query_ok, gathered / total, 0.0).astype(BF16))
    context[step] = jnp.concatenate(outs, axis=-1)

    @pl.when(step == pl.num_programs(0) - 1)
    def _():
        at_row = lax.broadcasted_iota(jnp.int32, (nearby, nearby), 0)
        at_lane = lax.broadcasted_iota(jnp.int32, (nearby, nearby), 1)
        natural = (at_lane % part) * DILATION_STEP + at_lane // part
        back = jnp.where(at_row == natural, 1.0, 0.0).astype(BF16)
        ordered = jnp.concatenate(
            [rows_ref[c, pl.ds(own, nearby), :] for c in range(seq_count)], axis=-1
        )
        emb_ref[...] = jnp.dot(back, ordered, preferred_element_type=F32).astype(BF16)
        whole = jnp.concatenate(
            [context[i] for i in range(HEAD_COUNT // STEP_HEADS)], axis=-1
        )
        whole = jnp.dot(back, whole, preferred_element_type=F32).astype(BF16)
        branch_ref[...] = jnp.dot(whole, wo_ref[...], preferred_element_type=F32).astype(BF16)


def attend(meta, rows, gain, weights, seq_count, nearby):
    width = STEP_HEADS * HEAD_WIDTH
    steps = HEAD_COUNT // STEP_HEADS
    slide_len = rows.shape[1]
    full = lambda *shape: pl.BlockSpec(shape, lambda i: (0,) * len(shape))
    out = jax.ShapeDtypeStruct((nearby, D), BF16)
    return pl.pallas_call(
        functools.partial(attention_kernel, seq_count, nearby),
        out_shape=(out, out),
        grid=(steps,),
        in_specs=[
            pl.BlockSpec(memory_space=pltpu.SMEM),
            full(*rows.shape),
            full(1, D),
            pl.BlockSpec((D, width), lambda i: (0, i)),
            pl.BlockSpec((D, width), lambda i: (0, steps + i)),
            pl.BlockSpec((D, width), lambda i: (0, 2 * steps + i)),
            pl.BlockSpec((D, D), lambda i: (0, 3)),
        ],
        out_specs=(full(nearby, D), full(nearby, D)),
        scratch_shapes=[
            pltpu.VMEM((slide_len, D), BF16),
            pltpu.VMEM((steps, nearby, width), BF16),
        ],
        compiler_params=pltpu.CompilerParams(vmem_limit_bytes=48 * 1024 * 1024),
        cost_estimate=pl.CostEstimate(
            flops=20_000_000_000, bytes_accessed=20_000_000, transcendentals=1_000_000
        ),
    )(meta, rows, gain, weights, weights, weights, weights)


def local(tile_feats, tile_pos, slide_count, w_proj, emb_grad, ln_gain, w_qkv, w_out):
    seq_count = lax.axis_size("seq")
    n = lax.axis_size("dp")
    seq_index = lax.axis_index("seq")
    slot_rows = tile_feats.shape[0]
    nearby = emb_grad.shape[1]
    slide_len = nearby * seq_count
    part = nearby // DILATION_STEP
    most = slot_rows // n
    width = w_proj.shape[1]
    weights = lax.all_gather(
        jnp.concatenate([w_qkv, w_out], axis=1), "dp", axis=0, tiled=True
    )
    positions, returned_grad = exchange(
        functools.partial(first_kernel, n, seq_count),
        1,
        [((n, 1, most), jnp.int32), ((seq_count, nearby, width), BF16)],
        [DMA((n,)), DMA((n,)), DMA((seq_count,)), DMA((seq_count,))],
        tile_pos.reshape(n, 1, most),
        emb_grad.reshape(nearby, seq_count, width).transpose(1, 0, 2),
    )
    positions = positions.reshape(slot_rows)
    spot = jnp.arange(slide_len, dtype=jnp.int32)
    hot = (spot[:, None] == positions[None, :]).astype(BF16)
    picked_grad = lax.dot_general(
        hot,
        returned_grad.reshape(slide_len, width),
        (((0,), (0,)), ((), ())),
        preferred_element_type=F32,
    ).astype(BF16)
    emb_part = jnp.dot(tile_feats, w_proj, preferred_element_type=F32).astype(BF16)
    arrived, slot_grad = exchange(
        functools.partial(second_kernel, n, seq_count),
        2,
        [((seq_count, n, most, width), BF16), ((n, most, width), BF16)],
        [DMA((n,))] * 4 + [DMA((seq_count, n))] * 2,
        emb_part.reshape(n, most, width),
        picked_grad.reshape(n, most, width),
    )
    grad_part = lax.dot_general(
        tile_feats,
        slot_grad.reshape(slot_rows, width),
        (((0,), (0,)), ((), ())),
        preferred_element_type=F32,
    ).astype(BF16)
    features = grad_part.shape[0]
    half = n // 2
    shape = (2, half, features // n, width)
    (summed,) = exchange(
        functools.partial(reduce_kernel, n),
        3,
        [(shape, BF16)],
        [pltpu.VMEM(shape[1:], BF16)] * 3 + [DMA((half,))] * 8,
        grad_part.reshape(shape),
    )
    proj_grad = summed.reshape(features, width).astype(F32)

    inside = spot % nearby
    at_spot = spot - inside + (inside % part) * DILATION_STEP + inside // part
    hot_perm = (at_spot[:, None] == positions[None, :]).astype(BF16)
    rows = jnp.einsum(
        "ps,csw->cpw",
        hot_perm,
        arrived.reshape(seq_count, slot_rows, width),
        preferred_element_type=F32,
    ).astype(BF16)
    meta = jnp.stack([seq_index.astype(jnp.int32), slide_count[0]])
    local_emb, attn_branch = attend(
        meta, rows, ln_gain.reshape(1, D), weights, seq_count, nearby
    )
    return (local_emb[None], attn_branch[None], proj_grad)


def solution(mesh):
    in_specs = (
        P("dp", None),
        P("dp", None),
        P("dp"),
        P(None, "seq"),
        P("dp", "seq", None),
        P(),
        P("dp", None),
        P("dp", None),
    )
    out_specs = (P("dp", "seq", None), P("dp", "seq", None), P(None, "seq"))
    return jax.shard_map(local, mesh=mesh, in_specs=in_specs, out_specs=out_specs, check_vma=False)
```

```python
import functools

import jax
import jax.numpy as jnp
from jax import lax
from jax.experimental import pallas as pl
from jax.experimental.pallas import tpu as pltpu
from jax.sharding import PartitionSpec as P

D = 768
HEAD_COUNT = 12
HEAD_WIDTH = 64
DILATION_STEP = 4
NEGATIVE = -1e30
EPSILON = 1e-05
STEP_HEADS = 4

F32 = jnp.float32
BF16 = jnp.bfloat16
MESH = pl.DeviceIdType.MESH


def greet(dp_peers, seq_peers):
    barrier = pltpu.get_barrier_semaphore()
    dp_count, seq_count = lax.axis_size("dp"), lax.axis_size("seq")
    dp, seq = lax.axis_index("dp"), lax.axis_index("seq")
    if dp_peers:

        @pl.loop(1, dp_count)
        def _(t):
            pl.semaphore_signal(
                barrier, device_id=(lax.rem(dp + t, dp_count), seq), device_id_type=MESH
            )

    if seq_peers:

        @pl.loop(1, seq_count)
        def _(t):
            pl.semaphore_signal(
                barrier, device_id=(dp, lax.rem(seq + t, seq_count)), device_id_type=MESH
            )

    pl.semaphore_wait(
        barrier, (dp_count - 1 if dp_peers else 0) + (seq_count - 1 if seq_peers else 0)
    )


def remote(src, dst, send, recv, device):
    return pltpu.make_async_remote_copy(
        src_ref=src,
        dst_ref=dst,
        send_sem=send,
        recv_sem=recv,
        device_id=device,
        device_id_type=MESH,
    )


def dispatch_kernel(
    n, seq_count, pos, grad, emb, pos_out, emb_out, grad_out, grad_rows, picked, *sems
):
    ps, pr, xs, xr, es, er, gs, gr, fs, fr = sems
    dp, seq = lax.axis_index("dp"), lax.axis_index("seq")
    most = pos.shape[2]
    nearby, width = grad.shape[1:]
    greet(True, True)

    def column_copy(t):
        peer = lax.rem(seq + t, seq_count)
        return remote(grad.at[peer], grad_rows.at[seq], xs.at[t], xr.at[t], (dp, peer))

    def pos_copy(t):
        peer = lax.rem(dp + t, n)
        return remote(pos.at[peer], pos_out.at[dp], ps.at[t], pr.at[t], (peer, seq))

    def emb_copy(t):
        peer = lax.rem(dp + t, n)
        return remote(emb.at[peer], emb_out.at[seq, dp], es.at[t], er.at[t], (peer, seq))

    def grad_copy(t):
        peer = lax.rem(dp + t, n)
        return remote(picked.at[peer], grad_out.at[dp], gs.at[t], gr.at[t], (peer, seq))

    def forward(k, t):
        source = lax.rem(dp - t + n, n)
        peer = lax.rem(seq + k, seq_count)
        block = emb_out.at[seq, source]
        return remote(block, block, fs.at[k, t], fr.at[k, t], (dp, peer))

    @pl.loop(1, seq_count)
    def _(t):
        column_copy(t).start()

    @pl.loop(1, n)
    def _(t):
        pos_copy(t).start()

    @pl.loop(1, n)
    def _(t):
        emb_copy(t).start()

    pos_out[dp] = pos[dp]
    grad_rows[seq] = grad[seq]
    emb_out[seq, dp] = emb[dp]

    @pl.loop(1, n)
    def _(t):
        pos_copy(t).wait()

    @pl.loop(1, seq_count)
    def _(t):
        column_copy(t).wait()

    rows = jnp.concatenate([grad_rows[i] for i in range(seq_count)], axis=0)
    spot = lax.broadcasted_iota(jnp.int32, (nearby * seq_count, 1), 0)
    batch = 4
    for first in range(0, n, batch):
        at = jnp.concatenate([pos_out[first + i] for i in range(batch)], axis=1)
        hot = jnp.where(spot == at, 1.0, 0.0).astype(BF16)
        block = lax.dot_general(
            hot, rows, (((0,), (0,)), ((), ())), preferred_element_type=F32
        ).astype(BF16)
        for i in range(batch):
            picked[first + i] = block[i * most : (i + 1) * most]

    @pl.loop(1, n)
    def _(t):
        grad_copy(t).start()

    grad_out[dp] = picked[dp]
    for k in range(1, seq_count):
        forward(k, 0).start()

    @pl.loop(1, n)
    def _(t):
        emb_copy(t).wait_recv()
        for k in range(1, seq_count):
            forward(k, t).start()

    @pl.loop(1, n)
    def _(t):
        emb_copy(t).wait_send()
        grad_copy(t).wait()

    @pl.loop(0, n)
    def _(t):
        for k in range(1, seq_count):
            forward(k, t).wait()


def reduce_kernel(n, src, out, pair, cross, stage_b, stage_c, arrive, *sems):
    s1, r1, s2, r2, s3, r3, s4, r4, s5, r5, s6, r6 = sems
    dp, seq = lax.axis_index("dp"), lax.axis_index("seq")
    q = n // 4
    a, b, c = lax.rem(dp, 2), lax.rem(dp // 2, 2), dp // 4
    sibling = (dp + 1 - 2 * a, seq)
    across = (dp + 2 - 4 * b, seq)
    barrier = pltpu.get_barrier_semaphore()
    pl.semaphore_signal(barrier, device_id=sibling, device_id_type=MESH)
    pl.semaphore_signal(barrier, device_id=across, device_id_type=MESH)

    def ahead(t):
        return lax.rem(c + t, q)

    def behind(t):
        return lax.rem(c - t + q, q)

    def along(t):
        return (ahead(t) * 4 + b * 2 + a, seq)

    @pl.loop(1, q)
    def _(t):
        pl.semaphore_signal(barrier, device_id=along(t), device_id_type=MESH)

    pl.semaphore_wait(barrier, q + 1)

    def side(i):
        return 1 - b if i == 0 else b

    def to_sibling(i, t):
        return remote(
            src.at[1 - a, side(i), ahead(t)], pair.at[i, t], s1.at[i, t], r1.at[i, t], sibling
        )

    def to_across(t):
        return remote(stage_b.at[t], cross.at[t], s2.at[t], r2.at[t], across)

    def to_owner(t):
        return remote(stage_c.at[t], arrive.at[t], s3.at[t], r3.at[t], along(t))

    def result_along(t):
        block = out.at[a, b, c]
        return remote(block, block, s4.at[t], r4.at[t], along(t))

    def result_across(t):
        block = out.at[a, b, behind(t)]
        return remote(block, block, s5.at[t], r5.at[t], across)

    def result_sibling(i, t):
        block = out.at[a, side(i), behind(t)]
        return remote(block, block, s6.at[i, t], r6.at[i, t], sibling)

    for i in (0, 1):

        @pl.loop(1, q + 1)
        def _(t):
            to_sibling(i, lax.rem(t, q)).start()

    @pl.loop(1, q + 1)
    def _(step):
        t = lax.rem(step, q)
        to_sibling(0, t).wait_recv()
        stage_b[t] = (src[a, 1 - b, ahead(t)].astype(F32) + pair[0, t].astype(F32)).astype(BF16)
        to_across(t).start()

    @pl.loop(1, q + 1)
    def _(step):
        t = lax.rem(step, q)
        to_sibling(1, t).wait_recv()
        to_across(t).wait_recv()
        stage_c[t] = (
            src[a, b, ahead(t)].astype(F32) + pair[1, t].astype(F32) + cross[t].astype(F32)
        ).astype(BF16)

        @pl.when(step < q)
        def _():
            to_owner(t).start()

    total = stage_c[0].astype(F32)
    for t in range(1, q):
        to_owner(t).wait_recv()
        total = total + arrive[t].astype(F32)
    out[a, b, c] = total.astype(BF16)

    @pl.loop(1, q)
    def _(t):
        result_along(t).start()

    result_across(0).start()
    result_sibling(1, 0).start()

    @pl.loop(1, q)
    def _(t):
        result_along(t).wait_recv()
        result_across(t).start()
        result_sibling(1, t).start()

    @pl.loop(0, q)
    def _(t):
        result_across(t).wait_recv()
        result_sibling(0, t).start()

    @pl.loop(1, q)
    def _(t):
        to_owner(t).wait_send()
        result_along(t).wait_send()

    for i in (0, 1):

        @pl.loop(0, q)
        def _(t):
            to_sibling(i, t).wait_send()
            result_sibling(i, t).wait()

    @pl.loop(0, q)
    def _(t):
        to_across(t).wait_send()
        result_across(t).wait_send()


VM = pl.BlockSpec(memory_space=pltpu.VMEM)
DMA = pltpu.SemaphoreType.DMA


def exchange(kernel, ident, outs, scratch, *operands):
    return pl.pallas_call(
        kernel,
        out_shape=tuple(jax.ShapeDtypeStruct(shape, kind) for shape, kind in outs),
        in_specs=[VM] * len(operands),
        out_specs=tuple([VM] * len(outs)),
        scratch_shapes=scratch,
        compiler_params=pltpu.CompilerParams(
            collective_id=ident, has_side_effects=True, vmem_limit_bytes=32 * 1024 * 1024
        ),
        cost_estimate=pl.CostEstimate(
            flops=10_000_000_000, bytes_accessed=10_000_000, transcendentals=0
        ),
    )(*operands)


def put_rows(whole, rows, low, high):
    pieces = [whole[:low]] if low else []
    pieces.append(rows)
    if high < whole.shape[0]:
        pieces.append(whole[high:])
    return jnp.concatenate(pieces, axis=0)


def attention_kernel(
    seq_count,
    nearby,
    meta_ref,
    rows_ref,
    gain_ref,
    wq_ref,
    wk_ref,
    wv_ref,
    wo_ref,
    emb_ref,
    branch_ref,
    normed,
    context,
):
    step = pl.program_id(0)
    me = meta_ref[0]
    count = meta_ref[1]
    part = nearby // DILATION_STEP
    own = pl.multiple_of(me * nearby, nearby)

    @pl.when(step == 0)
    def _():
        for block in range(seq_count):
            at = slice(block * nearby, (block + 1) * nearby)
            wide = jnp.concatenate(
                [rows_ref[c, at, :] for c in range(seq_count)], axis=-1
            ).astype(F32)
            center = jnp.mean(wide, axis=-1, keepdims=True)
            spread = jnp.mean(jnp.square(wide - center), axis=-1, keepdims=True)
            normed[at, :] = (
                (wide - center) * lax.rsqrt(spread + EPSILON) * gain_ref[...]
            ).astype(BF16)

    mine = normed[pl.ds(own, nearby), :]
    query = jnp.dot(mine, wq_ref[...], preferred_element_type=F32).astype(BF16)
    query = query * BF16(HEAD_WIDTH**-0.5)
    key = jnp.dot(mine, wk_ref[...], preferred_element_type=F32).astype(BF16)
    value = jnp.dot(mine, wv_ref[...], preferred_element_type=F32).astype(BF16)
    far_keys, far_values = [], []
    for other in range(1, seq_count):
        block = lax.rem(me + other, seq_count)
        start = pl.multiple_of(block * nearby, nearby)
        theirs = normed[pl.ds(start, nearby), :]
        far_keys.append(jnp.dot(theirs, wk_ref[...], preferred_element_type=F32).astype(BF16))
        far_values.append(jnp.dot(theirs, wv_ref[...], preferred_element_type=F32).astype(BF16))

    lane = lax.broadcasted_iota(jnp.int32, (1, nearby), 1)
    key_ok = own + (lane % part) * DILATION_STEP + lane // part < count
    row = lax.broadcasted_iota(jnp.int32, (nearby, 1), 0)
    query_ok = own + (row % part) * DILATION_STEP + row // part < count
    far_lane = lax.broadcasted_iota(jnp.int32, (1, part * (seq_count - 1)), 1)
    far_block = lax.rem(me + 1 + far_lane // part, seq_count)
    far_spot = far_block * nearby + far_lane % part * DILATION_STEP
    dims = (((1,), (1,)), ((), ()))
    outs = []
    for head in range(STEP_HEADS):
        shift = head % DILATION_STEP
        cols = slice(head * HEAD_WIDTH, (head + 1) * HEAD_WIDTH)
        low, high = shift * part, (shift + 1) * part
        q, k, v = query[:, cols], key[:, cols], value[:, cols]
        scores = lax.dot_general(q, k, dims, preferred_element_type=F32)
        scores = jnp.where(key_ok, scores, NEGATIVE)
        maximum = jnp.max(scores, axis=-1, keepdims=True)
        far_k = jnp.concatenate([x[low:high, cols] for x in far_keys], axis=0)
        far_v = jnp.concatenate([x[low:high, cols] for x in far_values], axis=0)
        far_ok = far_spot + shift < count
        far = lax.dot_general(q[low:high], far_k, dims, preferred_element_type=F32)
        far = jnp.where(far_ok, far, NEGATIVE)
        far_max = jnp.maximum(maximum[low:high], jnp.max(far, axis=-1, keepdims=True))
        maximum = put_rows(maximum, far_max, low, high)
        weight = jnp.exp(scores - maximum)
        in_lane = (lane >= low) & (lane < high)
        twice = jnp.where(in_lane, weight[low:high] * 2.0, weight[low:high])
        weight = put_rows(weight, twice, low, high)
        far_weight = jnp.exp(far - far_max)
        total = jnp.sum(weight, axis=-1, keepdims=True)
        far_total = jnp.sum(far_weight, axis=-1, keepdims=True)
        total = put_rows(total, total[low:high] + far_total, low, high)
        gathered = jnp.dot(weight.astype(BF16), v, preferred_element_type=F32)
        far_gathered = jnp.dot(far_weight.astype(BF16), far_v, preferred_element_type=F32)
        gathered = put_rows(gathered, gathered[low:high] + far_gathered, low, high)
        outs.append(jnp.where(query_ok, gathered / total, 0.0).astype(BF16))
    context[step] = jnp.concatenate(outs, axis=-1)

    @pl.when(step == pl.num_programs(0) - 1)
    def _():
        at_row = lax.broadcasted_iota(jnp.int32, (nearby, nearby), 0)
        at_lane = lax.broadcasted_iota(jnp.int32, (nearby, nearby), 1)
        natural = (at_lane % part) * DILATION_STEP + at_lane // part
        back = jnp.where(at_row == natural, 1.0, 0.0).astype(BF16)
        ordered = jnp.concatenate(
            [rows_ref[c, pl.ds(own, nearby), :] for c in range(seq_count)], axis=-1
        )
        emb_ref[...] = jnp.dot(back, ordered, preferred_element_type=F32).astype(BF16)
        whole = jnp.concatenate(
            [context[i] for i in range(HEAD_COUNT // STEP_HEADS)], axis=-1
        )
        whole = jnp.dot(back, whole, preferred_element_type=F32).astype(BF16)
        branch_ref[...] = jnp.dot(whole, wo_ref[...], preferred_element_type=F32).astype(BF16)


def attend(meta, rows, gain, weights, seq_count, nearby):
    width = STEP_HEADS * HEAD_WIDTH
    steps = HEAD_COUNT // STEP_HEADS
    slide_len = rows.shape[1]
    full = lambda *shape: pl.BlockSpec(shape, lambda i: (0,) * len(shape))
    out = jax.ShapeDtypeStruct((nearby, D), BF16)
    return pl.pallas_call(
        functools.partial(attention_kernel, seq_count, nearby),
        out_shape=(out, out),
        grid=(steps,),
        in_specs=[
            pl.BlockSpec(memory_space=pltpu.SMEM),
            full(*rows.shape),
            full(1, D),
            pl.BlockSpec((D, width), lambda i: (0, i)),
            pl.BlockSpec((D, width), lambda i: (0, steps + i)),
            pl.BlockSpec((D, width), lambda i: (0, 2 * steps + i)),
            pl.BlockSpec((D, D), lambda i: (0, 3)),
        ],
        out_specs=(full(nearby, D), full(nearby, D)),
        scratch_shapes=[
            pltpu.VMEM((slide_len, D), BF16),
            pltpu.VMEM((steps, nearby, width), BF16),
        ],
        compiler_params=pltpu.CompilerParams(vmem_limit_bytes=48 * 1024 * 1024),
        cost_estimate=pl.CostEstimate(
            flops=20_000_000_000, bytes_accessed=20_000_000, transcendentals=1_000_000
        ),
    )(meta, rows, gain, weights, weights, weights, weights)


def local(tile_feats, tile_pos, slide_count, w_proj, emb_grad, ln_gain, w_qkv, w_out):
    seq_count = lax.axis_size("seq")
    n = lax.axis_size("dp")
    seq_index = lax.axis_index("seq")
    slot_rows = tile_feats.shape[0]
    nearby = emb_grad.shape[1]
    slide_len = nearby * seq_count
    part = nearby // DILATION_STEP
    most = slot_rows // n
    width = w_proj.shape[1]
    weights = lax.all_gather(
        jnp.concatenate([w_qkv, w_out], axis=1), "dp", axis=0, tiled=True
    )
    emb_part = jnp.dot(tile_feats, w_proj, preferred_element_type=F32).astype(BF16)
    positions, arrived, slot_grad = exchange(
        functools.partial(dispatch_kernel, n, seq_count),
        1,
        [
            ((n, 1, most), jnp.int32),
            ((seq_count, n, most, width), BF16),
            ((n, most, width), BF16),
        ],
        [pltpu.VMEM((seq_count, nearby, width), BF16), pltpu.VMEM((n, most, width), BF16)]
        + [DMA((n,))] * 2
        + [DMA((seq_count,))] * 2
        + [DMA((n,))] * 4
        + [DMA((seq_count, n))] * 2,
        tile_pos.reshape(n, 1, most),
        emb_grad.reshape(nearby, seq_count, width).transpose(1, 0, 2),
        emb_part.reshape(n, most, width),
    )
    positions = positions.reshape(slot_rows)
    spot = jnp.arange(slide_len, dtype=jnp.int32)
    grad_part = lax.dot_general(
        tile_feats,
        slot_grad.reshape(slot_rows, width),
        (((0,), (0,)), ((), ())),
        preferred_element_type=F32,
    ).astype(BF16)
    features = grad_part.shape[0]
    quarter = n // 4
    shape = (2, 2, quarter, features // n, width)
    (summed,) = exchange(
        functools.partial(reduce_kernel, n),
        3,
        [(shape, BF16)],
        [pltpu.VMEM(shape[1:], BF16)]
        + [pltpu.VMEM(shape[2:], BF16)] * 4
        + [DMA((2, quarter))] * 2
        + [DMA((quarter,))] * 8
        + [DMA((2, quarter))] * 2,
        grad_part.reshape(shape),
    )
    proj_grad = summed.reshape(features, width).astype(F32)

    inside = spot % nearby
    at_spot = spot - inside + (inside % part) * DILATION_STEP + inside // part
    hot_perm = (at_spot[:, None] == positions[None, :]).astype(BF16)
    rows = jnp.einsum(
        "ps,csw->cpw",
        hot_perm,
        arrived.reshape(seq_count, slot_rows, width),
        preferred_element_type=F32,
    ).astype(BF16)
    meta = jnp.stack([seq_index.astype(jnp.int32), slide_count[0]])
    local_emb, attn_branch = attend(
        meta, rows, ln_gain.reshape(1, D), weights, seq_count, nearby
    )
    return (local_emb[None], attn_branch[None], proj_grad)


def solution(mesh):
    in_specs = (
        P("dp", None),
        P("dp", None),
        P("dp"),
        P(None, "seq"),
        P("dp", "seq", None),
        P(),
        P("dp", None),
        P("dp", None),
    )
    out_specs = (P("dp", "seq", None), P("dp", "seq", None), P(None, "seq"))
    return jax.shard_map(local, mesh=mesh, in_specs=in_specs, out_specs=out_specs, check_vma=False)
```

```python
import functools

import jax
import jax.numpy as jnp
from jax import lax
from jax.experimental import pallas as pl
from jax.experimental.pallas import tpu as pltpu
from jax.sharding import PartitionSpec as P

D = 768
HEAD_COUNT = 12
HEAD_WIDTH = 64
DILATION_STEP = 4
NEGATIVE = -1e30
EPSILON = 1e-05
STEP_HEADS = 4

F32 = jnp.float32
BF16 = jnp.bfloat16
MESH = pl.DeviceIdType.MESH


def greet(dp_peers, seq_peers):
    barrier = pltpu.get_barrier_semaphore()
    dp_count, seq_count = lax.axis_size("dp"), lax.axis_size("seq")
    dp, seq = lax.axis_index("dp"), lax.axis_index("seq")
    if dp_peers:

        @pl.loop(1, dp_count)
        def _(t):
            pl.semaphore_signal(
                barrier, device_id=(lax.rem(dp + t, dp_count), seq), device_id_type=MESH
            )

    if seq_peers:

        @pl.loop(1, seq_count)
        def _(t):
            pl.semaphore_signal(
                barrier, device_id=(dp, lax.rem(seq + t, seq_count)), device_id_type=MESH
            )

    pl.semaphore_wait(
        barrier, (dp_count - 1 if dp_peers else 0) + (seq_count - 1 if seq_peers else 0)
    )


def remote(src, dst, send, recv, device):
    return pltpu.make_async_remote_copy(
        src_ref=src,
        dst_ref=dst,
        send_sem=send,
        recv_sem=recv,
        device_id=device,
        device_id_type=MESH,
    )


def dispatch_kernel(
    n, seq_count, pos, grad, emb, pos_out, emb_out, grad_out, grad_rows, picked, *sems
):
    ps, pr, xs, xr, es, er, gs, gr, fs, fr = sems
    dp, seq = lax.axis_index("dp"), lax.axis_index("seq")
    most = pos.shape[2]
    nearby, width = grad.shape[1:]
    greet(True, True)

    def column_copy(t):
        peer = lax.rem(seq + t, seq_count)
        return remote(grad.at[peer], grad_rows.at[seq], xs.at[t], xr.at[t], (dp, peer))

    def pos_copy(t):
        peer = lax.rem(dp + t, n)
        return remote(pos.at[peer], pos_out.at[dp], ps.at[t], pr.at[t], (peer, seq))

    def emb_copy(t):
        peer = lax.rem(dp + t, n)
        return remote(emb.at[peer], emb_out.at[seq, dp], es.at[t], er.at[t], (peer, seq))

    def grad_copy(t):
        peer = lax.rem(dp + t, n)
        return remote(picked.at[peer], grad_out.at[dp], gs.at[t], gr.at[t], (peer, seq))

    def forward(k, t):
        source = lax.rem(dp - t + n, n)
        peer = lax.rem(seq + k, seq_count)
        block = emb_out.at[seq, source]
        return remote(block, block, fs.at[k, t], fr.at[k, t], (dp, peer))

    @pl.loop(1, seq_count)
    def _(t):
        column_copy(t).start()

    @pl.loop(1, n)
    def _(t):
        pos_copy(t).start()

    @pl.loop(1, n)
    def _(t):
        emb_copy(t).start()

    pos_out[dp] = pos[dp]
    grad_rows[seq] = grad[seq]
    emb_out[seq, dp] = emb[dp]

    @pl.loop(1, n)
    def _(t):
        pos_copy(t).wait()

    @pl.loop(1, seq_count)
    def _(t):
        column_copy(t).wait()

    rows = jnp.concatenate([grad_rows[i] for i in range(seq_count)], axis=0)
    spot = lax.broadcasted_iota(jnp.int32, (nearby * seq_count, 1), 0)
    batch = 4
    for first in range(0, n, batch):
        at = jnp.concatenate([pos_out[first + i] for i in range(batch)], axis=1)
        hot = jnp.where(spot == at, 1.0, 0.0).astype(BF16)
        block = lax.dot_general(
            hot, rows, (((0,), (0,)), ((), ())), preferred_element_type=F32
        ).astype(BF16)
        for i in range(batch):
            picked[first + i] = block[i * most : (i + 1) * most]

    @pl.loop(1, n)
    def _(t):
        grad_copy(t).start()

    grad_out[dp] = picked[dp]
    for k in range(1, seq_count):
        forward(k, 0).start()

    @pl.loop(1, n)
    def _(t):
        emb_copy(t).wait_recv()
        for k in range(1, seq_count):
            forward(k, t).start()

    @pl.loop(1, n)
    def _(t):
        emb_copy(t).wait_send()
        grad_copy(t).wait()

    @pl.loop(0, n)
    def _(t):
        for k in range(1, seq_count):
            forward(k, t).wait()


def reduce_kernel(n, feats, slots, out, src, pair, cross, stage_b, stage_c, arrive, *sems):
    s1, r1, s2, r2, s3, r3, s4, r4, s5, r5, s6, r6 = sems
    dp, seq = lax.axis_index("dp"), lax.axis_index("seq")
    q = n // 4
    a, b, c = lax.rem(dp, 2), lax.rem(dp // 2, 2), dp // 4
    sibling = (dp + 1 - 2 * a, seq)
    across = (dp + 2 - 4 * b, seq)
    barrier = pltpu.get_barrier_semaphore()
    pl.semaphore_signal(barrier, device_id=sibling, device_id_type=MESH)
    pl.semaphore_signal(barrier, device_id=across, device_id_type=MESH)

    def ahead(t):
        return lax.rem(c + t, q)

    def behind(t):
        return lax.rem(c - t + q, q)

    def along(t):
        return (ahead(t) * 4 + b * 2 + a, seq)

    @pl.loop(1, q)
    def _(t):
        pl.semaphore_signal(barrier, device_id=along(t), device_id_type=MESH)

    rows = src.shape[3]
    tile = 512
    for first in range(0, n * rows, tile):
        product = lax.dot_general(
            feats[:, first : first + tile],
            slots[...],
            (((0,), (0,)), ((), ())),
            preferred_element_type=F32,
        ).astype(BF16)
        for i in range(tile // rows):
            k = first // rows + i
            src[k // (2 * q), k // q % 2, k % q] = product[i * rows : (i + 1) * rows]

    pl.semaphore_wait(barrier, q + 1)

    def side(i):
        return 1 - b if i == 0 else b

    def to_sibling(i, t):
        return remote(
            src.at[1 - a, side(i), ahead(t)], pair.at[i, t], s1.at[i, t], r1.at[i, t], sibling
        )

    def to_across(t):
        return remote(stage_b.at[t], cross.at[t], s2.at[t], r2.at[t], across)

    def to_owner(t):
        return remote(stage_c.at[t], arrive.at[t], s3.at[t], r3.at[t], along(t))

    def result_along(t):
        block = out.at[a, b, c]
        return remote(block, block, s4.at[t], r4.at[t], along(t))

    def result_across(t):
        block = out.at[a, b, behind(t)]
        return remote(block, block, s5.at[t], r5.at[t], across)

    def result_sibling(i, t):
        block = out.at[a, side(i), behind(t)]
        return remote(block, block, s6.at[i, t], r6.at[i, t], sibling)

    for i in (0, 1):

        @pl.loop(1, q + 1)
        def _(t):
            to_sibling(i, lax.rem(t, q)).start()

    @pl.loop(1, q + 1)
    def _(step):
        t = lax.rem(step, q)
        to_sibling(0, t).wait_recv()
        stage_b[t] = (src[a, 1 - b, ahead(t)].astype(F32) + pair[0, t].astype(F32)).astype(BF16)
        to_across(t).start()

    @pl.loop(1, q + 1)
    def _(step):
        t = lax.rem(step, q)
        to_sibling(1, t).wait_recv()
        to_across(t).wait_recv()
        stage_c[t] = (
            src[a, b, ahead(t)].astype(F32) + pair[1, t].astype(F32) + cross[t].astype(F32)
        ).astype(BF16)

        @pl.when(step < q)
        def _():
            to_owner(t).start()

    total = stage_c[0].astype(F32)
    for t in range(1, q):
        to_owner(t).wait_recv()
        total = total + arrive[t].astype(F32)
    out[a, b, c] = total.astype(BF16)

    @pl.loop(1, q)
    def _(t):
        result_along(t).start()

    result_across(0).start()
    result_sibling(1, 0).start()

    @pl.loop(1, q)
    def _(t):
        result_along(t).wait_recv()
        result_across(t).start()
        result_sibling(1, t).start()

    @pl.loop(0, q)
    def _(t):
        result_across(t).wait_recv()
        result_sibling(0, t).start()

    @pl.loop(1, q)
    def _(t):
        to_owner(t).wait_send()
        result_along(t).wait_send()

    for i in (0, 1):

        @pl.loop(0, q)
        def _(t):
            to_sibling(i, t).wait_send()
            result_sibling(i, t).wait()

    @pl.loop(0, q)
    def _(t):
        to_across(t).wait_send()
        result_across(t).wait_send()


VM = pl.BlockSpec(memory_space=pltpu.VMEM)
DMA = pltpu.SemaphoreType.DMA


def exchange(kernel, ident, outs, scratch, *operands):
    return pl.pallas_call(
        kernel,
        out_shape=tuple(jax.ShapeDtypeStruct(shape, kind) for shape, kind in outs),
        in_specs=[VM] * len(operands),
        out_specs=tuple([VM] * len(outs)),
        scratch_shapes=scratch,
        compiler_params=pltpu.CompilerParams(
            collective_id=ident, has_side_effects=True, vmem_limit_bytes=32 * 1024 * 1024
        ),
        cost_estimate=pl.CostEstimate(
            flops=10_000_000_000, bytes_accessed=10_000_000, transcendentals=0
        ),
    )(*operands)


def put_rows(whole, rows, low, high):
    pieces = [whole[:low]] if low else []
    pieces.append(rows)
    if high < whole.shape[0]:
        pieces.append(whole[high:])
    return jnp.concatenate(pieces, axis=0)


def attention_kernel(
    seq_count,
    nearby,
    meta_ref,
    rows_ref,
    gain_ref,
    wq_ref,
    wk_ref,
    wv_ref,
    wo_ref,
    emb_ref,
    branch_ref,
    normed,
    context,
):
    step = pl.program_id(0)
    me = meta_ref[0]
    count = meta_ref[1]
    part = nearby // DILATION_STEP
    own = pl.multiple_of(me * nearby, nearby)

    @pl.when(step == 0)
    def _():
        for block in range(seq_count):
            at = slice(block * nearby, (block + 1) * nearby)
            wide = jnp.concatenate(
                [rows_ref[c, at, :] for c in range(seq_count)], axis=-1
            ).astype(F32)
            center = jnp.mean(wide, axis=-1, keepdims=True)
            spread = jnp.mean(jnp.square(wide - center), axis=-1, keepdims=True)
            normed[at, :] = (
                (wide - center) * lax.rsqrt(spread + EPSILON) * gain_ref[...]
            ).astype(BF16)

    mine = normed[pl.ds(own, nearby), :]
    query = jnp.dot(mine, wq_ref[...], preferred_element_type=F32).astype(BF16)
    query = query * BF16(HEAD_WIDTH**-0.5)
    key = jnp.dot(mine, wk_ref[...], preferred_element_type=F32).astype(BF16)
    value = jnp.dot(mine, wv_ref[...], preferred_element_type=F32).astype(BF16)
    far_keys, far_values = [], []
    for other in range(1, seq_count):
        block = lax.rem(me + other, seq_count)
        start = pl.multiple_of(block * nearby, nearby)
        theirs = normed[pl.ds(start, nearby), :]
        far_keys.append(jnp.dot(theirs, wk_ref[...], preferred_element_type=F32).astype(BF16))
        far_values.append(jnp.dot(theirs, wv_ref[...], preferred_element_type=F32).astype(BF16))

    lane = lax.broadcasted_iota(jnp.int32, (1, nearby), 1)
    key_ok = own + (lane % part) * DILATION_STEP + lane // part < count
    row = lax.broadcasted_iota(jnp.int32, (nearby, 1), 0)
    query_ok = own + (row % part) * DILATION_STEP + row // part < count
    far_lane = lax.broadcasted_iota(jnp.int32, (1, part * (seq_count - 1)), 1)
    far_block = lax.rem(me + 1 + far_lane // part, seq_count)
    far_spot = far_block * nearby + far_lane % part * DILATION_STEP
    dims = (((1,), (1,)), ((), ()))
    outs = []
    for head in range(STEP_HEADS):
        shift = head % DILATION_STEP
        cols = slice(head * HEAD_WIDTH, (head + 1) * HEAD_WIDTH)
        low, high = shift * part, (shift + 1) * part
        q, k, v = query[:, cols], key[:, cols], value[:, cols]
        scores = lax.dot_general(q, k, dims, preferred_element_type=F32)
        scores = jnp.where(key_ok, scores, NEGATIVE)
        maximum = jnp.max(scores, axis=-1, keepdims=True)
        far_k = jnp.concatenate([x[low:high, cols] for x in far_keys], axis=0)
        far_v = jnp.concatenate([x[low:high, cols] for x in far_values], axis=0)
        far_ok = far_spot + shift < count
        far = lax.dot_general(q[low:high], far_k, dims, preferred_element_type=F32)
        far = jnp.where(far_ok, far, NEGATIVE)
        far_max = jnp.maximum(maximum[low:high], jnp.max(far, axis=-1, keepdims=True))
        maximum = put_rows(maximum, far_max, low, high)
        weight = jnp.exp(scores - maximum)
        in_lane = (lane >= low) & (lane < high)
        twice = jnp.where(in_lane, weight[low:high] * 2.0, weight[low:high])
        weight = put_rows(weight, twice, low, high)
        far_weight = jnp.exp(far - far_max)
        total = jnp.sum(weight, axis=-1, keepdims=True)
        far_total = jnp.sum(far_weight, axis=-1, keepdims=True)
        total = put_rows(total, total[low:high] + far_total, low, high)
        gathered = jnp.dot(weight.astype(BF16), v, preferred_element_type=F32)
        far_gathered = jnp.dot(far_weight.astype(BF16), far_v, preferred_element_type=F32)
        gathered = put_rows(gathered, gathered[low:high] + far_gathered, low, high)
        outs.append(jnp.where(query_ok, gathered / total, 0.0).astype(BF16))
    context[step] = jnp.concatenate(outs, axis=-1)

    @pl.when(step == pl.num_programs(0) - 1)
    def _():
        at_row = lax.broadcasted_iota(jnp.int32, (nearby, nearby), 0)
        at_lane = lax.broadcasted_iota(jnp.int32, (nearby, nearby), 1)
        natural = (at_lane % part) * DILATION_STEP + at_lane // part
        back = jnp.where(at_row == natural, 1.0, 0.0).astype(BF16)
        ordered = jnp.concatenate(
            [rows_ref[c, pl.ds(own, nearby), :] for c in range(seq_count)], axis=-1
        )
        emb_ref[...] = jnp.dot(back, ordered, preferred_element_type=F32).astype(BF16)
        whole = jnp.concatenate(
            [context[i] for i in range(HEAD_COUNT // STEP_HEADS)], axis=-1
        )
        whole = jnp.dot(back, whole, preferred_element_type=F32).astype(BF16)
        branch_ref[...] = jnp.dot(whole, wo_ref[...], preferred_element_type=F32).astype(BF16)


def attend(meta, rows, gain, weights, seq_count, nearby):
    width = STEP_HEADS * HEAD_WIDTH
    steps = HEAD_COUNT // STEP_HEADS
    slide_len = rows.shape[1]
    full = lambda *shape: pl.BlockSpec(shape, lambda i: (0,) * len(shape))
    out = jax.ShapeDtypeStruct((nearby, D), BF16)
    return pl.pallas_call(
        functools.partial(attention_kernel, seq_count, nearby),
        out_shape=(out, out),
        grid=(steps,),
        in_specs=[
            pl.BlockSpec(memory_space=pltpu.SMEM),
            full(*rows.shape),
            full(1, D),
            pl.BlockSpec((D, width), lambda i: (0, i)),
            pl.BlockSpec((D, width), lambda i: (0, steps + i)),
            pl.BlockSpec((D, width), lambda i: (0, 2 * steps + i)),
            pl.BlockSpec((D, D), lambda i: (0, 3)),
        ],
        out_specs=(full(nearby, D), full(nearby, D)),
        scratch_shapes=[
            pltpu.VMEM((slide_len, D), BF16),
            pltpu.VMEM((steps, nearby, width), BF16),
        ],
        compiler_params=pltpu.CompilerParams(vmem_limit_bytes=60 * 1024 * 1024),
        cost_estimate=pl.CostEstimate(
            flops=20_000_000_000, bytes_accessed=20_000_000, transcendentals=1_000_000
        ),
    )(meta, rows, gain, weights, weights, weights, weights)


def local(tile_feats, tile_pos, slide_count, w_proj, emb_grad, ln_gain, w_qkv, w_out):
    seq_count = lax.axis_size("seq")
    n = lax.axis_size("dp")
    seq_index = lax.axis_index("seq")
    slot_rows = tile_feats.shape[0]
    nearby = emb_grad.shape[1]
    slide_len = nearby * seq_count
    part = nearby // DILATION_STEP
    most = slot_rows // n
    width = w_proj.shape[1]
    weights = lax.all_gather(
        jnp.concatenate([w_qkv, w_out], axis=1), "dp", axis=0, tiled=True
    )
    emb_part = jnp.dot(tile_feats, w_proj, preferred_element_type=F32).astype(BF16)
    positions, arrived, slot_grad = exchange(
        functools.partial(dispatch_kernel, n, seq_count),
        1,
        [
            ((n, 1, most), jnp.int32),
            ((seq_count, n, most, width), BF16),
            ((n, most, width), BF16),
        ],
        [pltpu.VMEM((seq_count, nearby, width), BF16), pltpu.VMEM((n, most, width), BF16)]
        + [DMA((n,))] * 2
        + [DMA((seq_count,))] * 2
        + [DMA((n,))] * 4
        + [DMA((seq_count, n))] * 2,
        tile_pos.reshape(n, 1, most),
        emb_grad.reshape(nearby, seq_count, width).transpose(1, 0, 2),
        emb_part.reshape(n, most, width),
    )
    positions = positions.reshape(slot_rows)
    spot = jnp.arange(slide_len, dtype=jnp.int32)
    features = tile_feats.shape[1]
    quarter = n // 4
    shape = (2, 2, quarter, features // n, width)
    (summed,) = exchange(
        functools.partial(reduce_kernel, n),
        3,
        [(shape, BF16)],
        [pltpu.VMEM(shape, BF16), pltpu.VMEM(shape[1:], BF16)]
        + [pltpu.VMEM(shape[2:], BF16)] * 4
        + [DMA((2, quarter))] * 2
        + [DMA((quarter,))] * 8
        + [DMA((2, quarter))] * 2,
        tile_feats,
        slot_grad.reshape(slot_rows, width),
    )
    proj_grad = summed.reshape(features, width).astype(F32)

    inside = spot % nearby
    at_spot = spot - inside + (inside % part) * DILATION_STEP + inside // part
    hot_perm = (at_spot[:, None] == positions[None, :]).astype(BF16)
    rows = jnp.einsum(
        "ps,csw->cpw",
        hot_perm,
        arrived.reshape(seq_count, slot_rows, width),
        preferred_element_type=F32,
    ).astype(BF16)
    meta = jnp.stack([seq_index.astype(jnp.int32), slide_count[0]])
    local_emb, attn_branch = attend(
        meta, rows, ln_gain.reshape(1, D), weights, seq_count, nearby
    )
    return (local_emb[None], attn_branch[None], proj_grad)


def solution(mesh):
    in_specs = (
        P("dp", None),
        P("dp", None),
        P("dp"),
        P(None, "seq"),
        P("dp", "seq", None),
        P(),
        P("dp", None),
        P("dp", None),
    )
    out_specs = (P("dp", "seq", None), P("dp", "seq", None), P(None, "seq"))
    return jax.shard_map(local, mesh=mesh, in_specs=in_specs, out_specs=out_specs, check_vma=False)
```
